256 devices in a mesh: prow: 32 (over x, z), pcol: 8 (over y, core).
Axes of the slice: x: 4, y: 4, z: 8, core: 2. Of those that a mesh axis runs over, the one named last changes fastest.
Arguments:
- matrix: float32 [2, 8192, 8, 2048], P(None, 'prow', None, 'pcol')
- pivots: int32 [512], replicated, may hold values from 0 to 16383, as said below
Outputs:
- factored: float32 [2, 8192, 8, 2048], P(None, 'prow', None, 'pcol')
The draws below stay inside these ranges and needn't reach their ends.
Inputs may be any that keep to these rules, and one draw needn't show every extreme that they name: For each panel k, the 256 entries pivots[k * 256 + s] are distinct, and each is either k * 256 + s or a row index of (k + 1) * 256 or more; each panel names the last row 16383 once and names at least one row of (k + 1) * 256 to (k + 2) * 256 - 1.
All inputs are finite; a program needn't handle non-finite values.
Results may differ from the reference program's by a relative error of at most 0.0001.
Values sent between devices are 32-bit elements; how exact they have to be, the bound alone decides.
No kernel may reach another device: no remote copies, remote signals or barrier semaphores. Data moves between devices by JAX's collectives and lax.ppermute only.
A program may use at most 192 MiB of HBM per device.

```python
import jax
import jax.numpy as jnp
from jax import lax

N = 16384
NB = 256
STEPS = 2
RBL = 2
CBL = 8
N_PROW = 32
N_PCOL = 8


def pivot_rows(key):
    pieces = []
    for panel_index in range(STEPS):
        subkey = jax.random.fold_in(key, 100 + panel_index)
        first_row = panel_index * NB
        span = N - first_row - NB
        shuffled = jax.random.permutation(jax.random.fold_in(subkey, 1), span).astype(jnp.int32)
        target = jax.random.randint(jax.random.fold_in(subkey, 2), (), 0, NB)
        shift = span - 1 - shuffled[target]
        shifted = (shuffled + shift) % span
        nearby = jax.random.randint(jax.random.fold_in(subkey, 4), (), 0, NB - 1).astype(jnp.int32)
        second = (target + 1 + jax.random.randint(jax.random.fold_in(subkey, 5), (), 0, NB - 1)) % NB
        where_near = jnp.argmax((shifted == nearby).astype(jnp.int32)).astype(jnp.int32)
        displaced = shifted[second]
        shifted = shifted.at[where_near].set(displaced).at[second].set(nearby)
        faraway = shifted[:NB] + first_row + NB
        offsets = jnp.arange(NB, dtype=jnp.int32)
        staying = (jax.random.randint(jax.random.fold_in(subkey, 3), (NB,), 0, 8) == 0) & (offsets != target) & (offsets != second)
        pieces.append(jnp.where(staying, first_row + offsets, faraway))
    return jnp.concatenate(pieces).astype(jnp.int32)


def draw_pivots(key, part):
    return pivot_rows(key)


def draw_matrix(key, part):
    chosen = pivot_rows(key)
    key = jax.random.fold_in(key, 7)
    key_off = jax.random.fold_in(key, 1)
    key_size = jax.random.fold_in(key, 2)
    key_sign = jax.random.fold_in(key, 3)
    offdiag = jnp.clip(jax.random.normal(key_off, (N, N), jnp.float32), -4.0, 4.0)
    scale = 2.0 * float(NB) ** 0.5
    magnitude = jax.random.uniform(key_size, (N,), jnp.float32, 1.0, 2.0) * scale
    signs = jnp.where(jax.random.randint(key_sign, (N,), 0, 2) == 0, -1.0, 1.0).astype(jnp.float32)
    indices = jnp.arange(N, dtype=jnp.int32)
    diagonal = indices[:, None] == indices[None, :]
    settled = jnp.where(diagonal, (signs * magnitude)[:, None], offdiag)
    placing = indices
    for panel_index in range(STEPS):
        first_row = panel_index * NB
        top_index = first_row + jnp.arange(NB, dtype=jnp.int32)
        picked = chosen[first_row:first_row + NB]
        from_top = placing[top_index]
        from_far = placing[picked]
        placing = placing.at[picked].set(from_top).at[top_index].set(from_far)
    result = jnp.zeros((N, N), jnp.float32).at[placing].set(settled)
    return result.reshape(RBL, N_PROW * NB, CBL, N_PCOL * NB)


def setup_inputs(seed: int = 0) -> dict:
    key_of = jax.random.split(jax.random.key(seed), 3)
    return {
        "matrix": draw_matrix(jax.random.fold_in(key_of[2], 71), 0),
        "pivots": draw_pivots(jax.random.fold_in(key_of[2], 71), 0),
    }


def product(former, latter):
    return jnp.dot(former, latter, precision=lax.Precision.HIGHEST, preferred_element_type=jnp.float32)


def factor(square):
    size = square.shape[0]
    if size == 1:
        return square, jnp.ones_like(square), 1.0 / square
    half_size = size // 2
    first_packed, first_lower, first_upper = factor(square[:half_size, :half_size])
    upper_right = product(first_lower, square[:half_size, half_size:])
    lower_left = product(square[half_size:, :half_size], first_upper)
    remainder = square[half_size:, half_size:] - product(lower_left, upper_right)
    second_packed, second_lower, second_upper = factor(remainder)
    empty = jnp.zeros((half_size, half_size), jnp.float32)
    packed = jnp.concatenate([jnp.concatenate([first_packed, upper_right], 1), jnp.concatenate([lower_left, second_packed], 1)], 0)
    lower_corner = -product(second_lower, product(lower_left, first_lower))
    lower_inv = jnp.concatenate([jnp.concatenate([first_lower, empty], 1), jnp.concatenate([lower_corner, second_lower], 1)], 0)
    upper_corner = -product(first_upper, product(upper_right, second_upper))
    upper_inv = jnp.concatenate([jnp.concatenate([first_upper, upper_corner], 1), jnp.concatenate([empty, second_upper], 1)], 0)
    return packed, lower_inv, upper_inv


def reference(matrix, pivots):
    current = matrix.reshape(N, N)
    for panel_index in range(STEPS):
        first_row = panel_index * NB
        last_row = first_row + NB
        chosen = pivots[first_row:last_row].astype(jnp.int32)
        top_rows = current[first_row:last_row, first_row:]
        far_rows = jnp.take(current[:, first_row:], chosen, axis=0)
        current = current.at[chosen, first_row:].set(top_rows)
        current = current.at[first_row:last_row, first_row:].set(far_rows)
        packed, lower_inv, upper_inv = factor(current[first_row:last_row, first_row:last_row])
        lower_part = product(current[last_row:, first_row:last_row], upper_inv)
        upper_part = product(lower_inv, current[first_row:last_row, last_row:])
        trailing = current[last_row:, last_row:] - product(lower_part, upper_part)
        current = current.at[first_row:last_row, first_row:last_row].set(packed)
        current = current.at[last_row:, first_row:last_row].set(lower_part)
        current = current.at[first_row:last_row, last_row:].set(upper_part)
        current = current.at[last_row:, last_row:].set(trailing)
    return current.reshape(RBL, N_PROW * NB, CBL, N_PCOL * NB)
```

```python
import jax
import jax.numpy as jnp
from jax import lax
from jax.experimental import pallas as pl
from jax.experimental.pallas import tpu as pltpu
from jax.sharding import PartitionSpec as P

BASE = 64
GROUP = 8
LIMIT = 48 * 2**20


def exact(a, b):
    return jnp.dot(a, b, precision=lax.Precision.HIGHEST, preferred_element_type=jnp.float32)


def split(a):
    high = a.astype(jnp.bfloat16)
    return high, (a - high.astype(jnp.float32)).astype(jnp.bfloat16)


def triple(a, b):
    dot = lambda x, y: jnp.dot(x, y, preferred_element_type=jnp.float32)
    return dot(a[0], b[0]) + (dot(a[0], b[1]) + dot(a[1], b[0]))


def factor_base(block):
    n = BASE
    tiles = n // 8
    lane = lax.broadcasted_iota(jnp.int32, (8, 128), 1)
    sub = lax.broadcasted_iota(jnp.int32, (8, 128), 0)
    row_id = lax.broadcasted_iota(jnp.int32, (n, n), 0)
    col_id = lax.broadcasted_iota(jnp.int32, (n, n), 1)
    unit = jnp.where(row_id == col_id, 1.0, 0.0).astype(jnp.float32)
    wide = [jnp.concatenate([block, unit], 1), jnp.concatenate([block.T, unit], 1)]
    work = [[w[8 * r:8 * r + 8] for r in range(tiles)] for w in wide]
    lower = [jnp.zeros((8, 128), jnp.float32) for _ in range(tiles)]
    scale = [jnp.zeros((8, 128), jnp.float32) for _ in range(tiles)]
    spread = lambda tile, s: jnp.broadcast_to(tile[s:s + 1, :], (8, 128))
    for first in range(0, n, GROUP):
        cols = [
            {j: {r: jnp.broadcast_to(work[b][r][:, j:j + 1], (8, 128)) for r in range(first // 8, tiles)}
             for j in range(first, first + GROUP)}
            for b in range(2)
        ]
        for k in range(first, first + GROUP):
            kt, ks = divmod(k, 8)
            for b in range(2):
                inv = 1.0 / spread(cols[b][k][kt], ks)
                mult = {r: cols[b][k][r] * inv for r in range(kt, tiles)}
                mult[kt] = jnp.where(sub > ks, mult[kt], 0.0)
                for j in range(k + 1, first + GROUP):
                    across = spread(cols[b][j][kt], ks)
                    for r in range(kt, tiles):
                        cols[b][j][r] = cols[b][j][r] - mult[r] * across
                across = spread(work[b][kt], ks)
                for r in range(kt, tiles):
                    work[b][r] = work[b][r] - mult[r] * across
                if b == 0:
                    for r in range(kt, tiles):
                        lower[r] = jnp.where(lane == k, mult[r], lower[r])
                else:
                    scale[kt] = jnp.where(sub == ks, inv, scale[kt])
    first_work = jnp.concatenate(work[0], 0)
    second_work = jnp.concatenate([work[1][r] * scale[r] for r in range(tiles)], 0)
    packed = jnp.where(row_id <= col_id, first_work[:, :n], jnp.concatenate(lower, 0)[:, :n])
    lower_inv = first_work[:, n:]
    upper_inv = second_work[:, n:].T
    return packed, lower_inv, upper_inv

def join(a, b, c, d):
    return jnp.concatenate([jnp.concatenate([a, b], 1), jnp.concatenate([c, d], 1)], 0)

def factor(square):
    size = square.shape[0]
    if size == BASE:
        return factor_base(square)
    h = size // 2
    p1, l1, u1 = factor(square[:h, :h])
    ur = exact(l1, square[:h, h:])
    ll = exact(square[h:, :h], u1)
    p2, l2, u2 = factor(square[h:, h:] - exact(ll, ur))
    z = jnp.zeros((h, h), jnp.float32)
    return (join(p1, ur, ll, p2), join(l1, z, -exact(l2, exact(ll, l1)), l2),
            join(u1, -exact(u1, exact(ur, u2)), z, u2))

def factor_kernel(d_ref, packed_ref, linv_ref, uinv_ref):
    h = d_ref.shape[0] // 2
    p1, l1, u1 = factor(d_ref[:h, :h])
    ur = exact(l1, d_ref[:h, h:])
    ll = exact(d_ref[h:, :h], u1)
    packed_ref[:h, :h] = p1
    packed_ref[:h, h:] = ur
    packed_ref[h:, :h] = ll
    linv_ref[0] = l1
    uinv_ref[0] = u1
    p2, l2, u2 = factor(d_ref[h:, h:] - exact(ll, ur))
    packed_ref[h:, h:] = p2
    linv_ref[1] = l2
    uinv_ref[1] = u2

def assemble_and_factor(
    me_ref, own_ref, other_ref, packed_ref, linv_ref, uinv_ref, square,
):
    per, rows = own_ref.shape[0], own_ref.shape[1]
    for core, ref in ((0, own_ref), (1, other_ref)):
        for turn in range(per):
            segment = lax.rem(me_ref[1] // 2 + turn, per) * 2 + lax.rem(me_ref[1] + core, 2)
            at = pl.ds(pl.multiple_of(segment * rows, rows), rows)
            square[at, :] = ref[turn]
    factor_kernel(square, packed_ref, linv_ref, uinv_ref)


def factor_two(me, own, other):
    n = own.shape[2]
    half = jax.ShapeDtypeStruct((2, n // 2, n // 2), jnp.float32)
    smem = pl.BlockSpec(memory_space=pltpu.SMEM)
    vmem = pl.BlockSpec(memory_space=pltpu.VMEM)
    return pl.pallas_call(
        assemble_and_factor,
        out_shape=(jax.ShapeDtypeStruct((n, n), jnp.float32), half, half),
        in_specs=[smem, vmem, vmem],
        out_specs=(vmem, vmem, vmem),
        scratch_shapes=[pltpu.VMEM((n, n), jnp.float32)],
        compiler_params=pltpu.CompilerParams(vmem_limit_bytes=LIMIT),
        cost_estimate=pl.CostEstimate(
            flops=20_000_000_000, bytes_accessed=3 * 2**20, transcendentals=0
        ),
    )(me, own, other)


def panels_kernel(
    me_ref, src_ref, raw_ref, own_ref, other_ref, packed_ref, uinv_ref, store_ref, high_ref,
    low_ref, tops_ref,
):
    n = raw_ref.shape[0]
    h = n // 2
    per, rows = own_ref.shape[0], own_ref.shape[1]
    for core, ref in ((0, own_ref), (1, other_ref)):
        for turn in range(per):
            segment = lax.rem(me_ref[1] // 2 + turn, per) * 2 + lax.rem(me_ref[1] + core, 2)
            at = pl.ds(pl.multiple_of(segment * rows, rows), rows)
            tops_ref[at, :] = ref[turn]
    src = src_ref[...]
    row = src[:, 0:1]
    moved = src[:, 1:2]
    moved_first = src[:, 2:3]
    column = lax.broadcasted_iota(jnp.int32, (n, n), 1)
    pick = jnp.where((moved == column) & (moved != row), 1.0, 0.0).astype(jnp.float32)
    raw = raw_ref[...]
    both = jnp.where(moved != row, exact(pick, tops_ref[...]), raw)
    pick = jnp.where((moved_first == column) & (moved_first != row), 1.0, 0.0)[:, :h]
    first = jnp.where(
        moved_first != row, exact(pick.astype(jnp.float32), tops_ref[:h, :h]), raw[:, :h]
    )
    store_ref[0] = exact(first, uinv_ref[0])
    left = exact(both[:, :h], uinv_ref[0])
    right = exact(both[:, h:] - exact(left, packed_ref[:h, h:]), uinv_ref[1])
    store_ref[1] = right
    high, low = split(jnp.concatenate([left, right], 1))
    high_ref[...] = high
    low_ref[...] = low


def panels(me, src, raw, own, other, packed, uinv):
    n = raw.shape[0]
    pair = jax.ShapeDtypeStruct((n, n), jnp.bfloat16)
    smem = pl.BlockSpec(memory_space=pltpu.SMEM)
    vmem = pl.BlockSpec(memory_space=pltpu.VMEM)
    return pl.pallas_call(
        panels_kernel,
        out_shape=(jax.ShapeDtypeStruct((2, n, n // 2), jnp.float32), pair, pair),
        in_specs=[smem] + [vmem] * 6,
        out_specs=(vmem, vmem, vmem),
        scratch_shapes=[pltpu.VMEM((n, n), jnp.float32)],
        compiler_params=pltpu.CompilerParams(vmem_limit_bytes=LIMIT),
        cost_estimate=pl.CostEstimate(
            flops=5_000_000_000, bytes_accessed=6 * 2**20, transcendentals=0
        ),
    )(me, src, raw, own, other, packed, uinv)


def pick_kernel(index_ref, raw_ref, *out_refs):
    rows, depth = index_ref.shape[0], raw_ref.shape[0]
    column = lax.broadcasted_iota(jnp.int32, (rows, depth), 1)
    pick = jnp.where(index_ref[...] == column, 1.0, 0.0).astype(jnp.float32)
    picked = exact(pick, raw_ref[...])
    step = rows // len(out_refs)
    for k, ref in enumerate(out_refs):
        ref[...] = picked[k * step : (k + 1) * step]


def pick_pieces(index, raw, pieces):
    shape = jax.ShapeDtypeStruct((index.shape[0] // pieces, raw.shape[1]), jnp.float32)
    return pl.pallas_call(
        pick_kernel,
        out_shape=(shape,) * pieces,
        compiler_params=pltpu.CompilerParams(vmem_limit_bytes=LIMIT),
    )(index, raw)


def fetch_kernel(local_ref, mine_ref, out_ref, sem):
    copies = [
        pltpu.make_async_copy(mine_ref.at[local_ref[k]], out_ref.at[k], sem.at[k])
        for k in range(out_ref.shape[0])
    ]
    for copy in copies:
        copy.start()
    for copy in copies:
        copy.wait()


def fetch(local, mine):
    count = local.shape[0]
    hbm = pl.BlockSpec(memory_space=pl.ANY)
    return pl.pallas_call(
        fetch_kernel,
        out_shape=jax.ShapeDtypeStruct((count,) + mine.shape[1:], jnp.float32),
        in_specs=[pl.BlockSpec(memory_space=pltpu.SMEM), hbm],
        out_specs=hbm,
        scratch_shapes=[pltpu.SemaphoreType.DMA((count,))],
    )(local, mine)


def collect_kernel(local_ref, mine_ref, out_ref):
    def one(s, _):
        at = local_ref[s]

        @pl.when(at >= 0)
        def _():
            out_ref[s] = mine_ref[at]

        @pl.when(at < 0)
        def _():
            out_ref[s] = jnp.zeros_like(out_ref[s])

        return 0

    lax.fori_loop(0, local_ref.shape[0], one, 0)


def collect(local, mine):
    vmem = pl.BlockSpec(memory_space=pltpu.VMEM)
    return pl.pallas_call(
        collect_kernel,
        out_shape=jax.ShapeDtypeStruct((local.shape[0],) + mine.shape[1:], jnp.float32),
        in_specs=[pl.BlockSpec(memory_space=pltpu.SMEM), vmem],
        out_specs=vmem,
        compiler_params=pltpu.CompilerParams(vmem_limit_bytes=LIMIT),
    )(local, mine)


def trailing_kernel(
    cols, me_ref, row_ref, src_ref, at_ref, *refs,
):
    pieces, (
        far_ref, mine_ref, high_ref, low_ref, packed_ref, linv_ref, store_ref, out_ref, work, top,
        right_high, right_low, far, old_ref, in_sem, top_sem, out_sem,
    ) = refs[:-17], refs[-17:]
    rows = row_ref.shape[0]
    h = rows // 2
    lanes = top.shape[2]
    halves = range(top.shape[0])
    part = lambda i: pl.ds(i * lanes, lanes)
    top_copies = [pltpu.make_async_copy(far_ref, far, top_sem.at[len(pieces)])]
    place = 0
    for k, piece in enumerate(pieces):
        count = piece.shape[0]
        top_copies.append(
            pltpu.make_async_copy(piece, old_ref.at[pl.ds(place, count)], top_sem.at[k])
        )
        place += count
    in_copies = [
        pltpu.make_async_copy(mine_ref.at[:, part(i)], work.at[i], in_sem.at[i]) for i in halves
    ]
    for copy in top_copies + in_copies:
        copy.start()

    def load(ref, first, count, j):
        at = pl.ds(first * cols + j, count, stride=cols)
        return jnp.concatenate([ref[i, at, :] for i in halves], 1)

    def store(ref, first, count, j, value):
        at = pl.ds(first * cols + j, count, stride=cols)
        for i in halves:
            ref[i, at, :] = value[:, i * lanes : (i + 1) * lanes]

    inverse = [split(linv_ref[k]) for k in range(2)]
    corner = split(packed_ref[h:, :h])
    my_row = me_ref[0]
    my_col = me_ref[1]
    for copy in top_copies:
        copy.wait()

    def bring(t, _):
        source = at_ref[t]
        target = pl.ds(pl.multiple_of(t * cols, cols), cols)

        @pl.when(source < rows)
        def _():
            at = pl.ds(pl.multiple_of(source * cols, cols), cols)
            for i in halves:
                top[i, target, :] = old_ref[at, part(i)]

        @pl.when(source >= rows)
        def _():
            at = pl.ds(pl.multiple_of((source - rows) * cols, cols), cols)
            for i in halves:
                top[i, target, :] = far[at, part(i)]

        return 0

    lax.fori_loop(0, rows, bring, 0)
    for j in range(cols):
        upper = triple(inverse[0], split(load(top, 0, h, j)))
        upper_pair = split(upper)
        second = load(top, h, h, j) - triple(corner, upper_pair)
        second = triple(inverse[1], split(second))
        second_pair = split(second)
        store(top, 0, h, j, upper)
        store(top, h, h, j, second)
        for ref, pieces in ((right_high, (upper_pair[0], second_pair[0])),
                            (right_low, (upper_pair[1], second_pair[1]))):
            for k, piece in enumerate(pieces):
                ref[j, k * h : k * h + h, :] = piece
    for copy in in_copies:
        copy.wait()

    def land(t, _):
        source = src_ref[t]

        @pl.when(source >= 0)
        def _():
            target = pl.ds(pl.multiple_of(t * cols, cols), cols)
            at = pl.ds(pl.multiple_of(source * cols, cols), cols)
            for i in halves:
                work[i, target, :] = old_ref[at, part(i)]

        return 0

    lax.fori_loop(0, rows, land, 0)
    out_copies = []
    for first in range(0, rows, h):
        at = slice(first, first + h)
        for j in range(cols):
            update = triple(
                (high_ref[at, :], low_ref[at, :]), (right_high[j], right_low[j])
            )
            store(work, first, h, j, load(work, first, h, j) - update)
        if first == 0:
            for k in range(2):

                @pl.when(my_row == k)
                def _():
                    work[:, : h * cols, :] = top[:, k * h * cols : (k + 1) * h * cols, :]

        for k in range(2):

            @pl.when(my_col == k)
            def _():
                store(work, first, h, 0, store_ref[k, at, :])
                if first == 0:
                    for i in range(k + 1):

                        @pl.when(my_row == i)
                        def _():
                            store(
                                work, 0, h, 0,
                                packed_ref[i * h : i * h + h, k * h : k * h + h],
                            )

        span = pl.ds(first * cols, h * cols)
        for i in halves:
            copy = pltpu.make_async_copy(
                work.at[i, span], out_ref.at[span, part(i)], out_sem.at[i, first // h]
            )
            copy.start()
            out_copies.append(copy)
    for copy in out_copies:
        copy.wait()


def trailing(me, row, src, at, pieces, far, mine, high, low, packed, linv, store, cols):
    smem = pl.BlockSpec(memory_space=pltpu.SMEM)
    vmem = pl.BlockSpec(memory_space=pltpu.VMEM)
    hbm = pl.BlockSpec(memory_space=pl.ANY)
    rows = row.shape[0]
    width = mine.shape[1]
    wide = pltpu.VMEM((width // 128, rows * cols, 128), jnp.float32)
    right = pltpu.VMEM((cols, rows, width), jnp.bfloat16)
    body = lambda *refs: trailing_kernel(cols, *refs)
    return pl.pallas_call(
        body,
        out_shape=jax.ShapeDtypeStruct(mine.shape, jnp.float32),
        in_specs=[smem] * 4 + [hbm] * (len(pieces) + 2) + [vmem] * 5,
        out_specs=hbm,
        scratch_shapes=[
            wide, wide, right, right,
            pltpu.VMEM(far.shape, jnp.float32),
            pltpu.VMEM(mine.shape, jnp.float32),
            pltpu.SemaphoreType.DMA((2,)),
            pltpu.SemaphoreType.DMA((len(pieces) + 1,)),
            pltpu.SemaphoreType.DMA((2, 2)),
        ],
        compiler_params=pltpu.CompilerParams(vmem_limit_bytes=LIMIT),
    )(me, row, src, at, *pieces, far, mine, high, low, packed, linv, store)


def spread_columns(first, my_col):
    step = [lax.ppermute(first, "pcol", pairs) for pairs in ([(0, 2), (1, 3)], [(0, 6), (1, 7)])]
    held = jnp.where(my_col < 2, first, step[0] + step[1])
    last = lax.ppermute(held, "pcol", [(2, 4), (7, 5)])
    held = jnp.where((my_col == 4) | (my_col == 5), last, held)
    other = lax.ppermute(held, "pcol", [(i, i ^ 1) for i in range(8)])
    even = my_col % 2 == 0
    return jnp.concatenate([jnp.where(even, held, other), jnp.where(even, other, held)], 1)


SLOTS = 32
X, Z, Y = 4, 8, 4


def along_z(value, turn, starts=range(Z)):
    pairs = [(x * Z + z, x * Z + (z + turn) % Z) for x in range(X) for z in starts]
    return lax.ppermute(value, "prow", pairs)


def along_x(value, turn):
    pairs = [(x * Z + z, (x + turn) % X * Z + z) for x in range(X) for z in range(Z)]
    return lax.ppermute(value, "prow", pairs)


def gather_segments(piece, my_col):
    held = [piece] + [
        lax.ppermute(piece, "pcol", [((q + 2 * k) % 8, q) for q in range(8)]) for k in range(1, Y)
    ]
    own = jnp.stack(held)
    return own, lax.ppermute(own, "pcol", [(q, q ^ 1) for q in range(8)])


def total_over_rows(value, distances):
    for d in distances:
        value = value + lax.ppermute(value, "prow", [(i, i ^ d) for i in range(X * Z)])
    return value


def spread_tops(tops, my_row):
    per = tops.shape[0] // (X * Z)
    plane = per * Z
    x, z = my_row // Z, my_row % Z
    sent = [
        lax.ppermute(tops[k * plane : (k + 1) * plane], "prow", [(0, k * Z), (1, k * Z + 1)])
        for k in range(1, X)
    ]
    held = jnp.where(x == 0, tops[:plane], sum(sent))
    held = jnp.where(z == 1, jnp.concatenate([held[per:], held[:per]], 0), held)
    chunks = [held[k * per : (k + 1) * per] for k in range(Z)]
    sent = [chunks[0]] + [along_z(chunks[k], k, range(2)) for k in range(1, Z)]
    chosen = []
    for start in range(2):
        total = jnp.zeros_like(chunks[0])
        for k in range(Z):
            total = total + jnp.where(z == (start + k) % Z, sent[k], 0.0)
        chosen.append(total)
    chunk = jnp.concatenate(chosen, 0)
    block = jnp.concatenate([chunk] + [along_z(chunk, k) for k in range(1, Z)], 0)
    left = along_x(block, 1)
    right = along_x(block, -1)
    half = block.shape[0] // 2
    return block, left, right, along_x(left[:half], 1), along_x(right[half:], -1)


def place_of_top(index, my_row, block):
    per = block // (X * Z)
    x, z = my_row // Z, my_row % Z
    owner = index % block // per
    away = (owner // Z - x) % X
    base = jnp.where(away == 0, 0, jnp.where(away == X - 1, 1, jnp.where(away == 1, 2, 3)))
    turn = (z - owner % Z) % Z
    return base * (2 * per * Z) + turn * (2 * per) + index // block * per + index % per


def per_device(matrix, pivots):
    prow_count = lax.axis_size("prow")
    pcol_count = lax.axis_size("pcol")
    my_row = lax.axis_index("prow")
    my_col = lax.axis_index("pcol")
    row_count, block, cols, width = matrix.shape
    rows = row_count * block
    mine = matrix.reshape(rows, cols, width)
    me = jnp.stack([my_row, my_col]).astype(jnp.int32)
    offsets = jnp.arange(block, dtype=jnp.int32)
    row = (
        (jnp.arange(row_count, dtype=jnp.int32) * prow_count + my_row)[:, None] * block
        + offsets[None, :]
    ).reshape(rows)
    first_pivots = pivots[:block]
    second_pivots = pivots[block:]
    count = 2 * block

    def exchanged(index, chosen, start):
        match = (index[:, None] == chosen[None, :]) & (index[:, None] >= start + block)
        found = jnp.max(jnp.where(match, offsets[None, :] + start, -1), axis=1)
        return jnp.where(found >= 0, found, index)

    source = jnp.concatenate([first_pivots, exchanged(second_pivots, first_pivots, 0)])
    panel = source // block
    holder = panel % prow_count
    place = panel // prow_count * block + source % block
    local = jnp.where(holder == my_row, place, -1)
    far = source >= count
    order = jnp.arange(count, dtype=jnp.int32)
    before = (holder[:, None] == holder[None, :]) & far[None, :] & (order[None, :] < order[:, None])
    rank = jnp.sum(before.astype(jnp.int32), axis=1)
    fits = jnp.max(jnp.where(far, rank, 0)) < SLOTS
    slots = jnp.arange(SLOTS, dtype=jnp.int32)
    filled = (rank[None, :] == slots[:, None]) & (far & (holder == my_row))[None, :]
    wanted = jnp.sum(jnp.where(filled, place[None, :], 0), axis=1)
    sent = fetch(wanted, mine)
    gathered = lax.all_gather(sent, "prow", tiled=True)

    first = mine[:, 0, :]
    segment = count // pcol_count
    tops_local = jnp.where(order // block == my_row, order % block, -1)
    both = jnp.stack([local, tops_local], 0).reshape(2, pcol_count, segment)
    turned = jnp.take(both, (my_col + jnp.arange(pcol_count)) % pcol_count, axis=1)
    index = turned.transpose(1, 0, 2).reshape(2 * count, 1)
    pieces = pick_pieces(index, first, pcol_count)
    moved_pieces = [pieces[0]] + [
        lax.ppermute(pieces[k], "pcol", [(0, k), (1, (1 + k) % pcol_count)])
        for k in range(1, pcol_count)
    ]
    sides = []
    for start in range(2):
        total = jnp.zeros_like(pieces[0])
        for k in range(pcol_count):
            here = my_col == (start + k) % pcol_count
            total = total + jnp.where(here, moved_pieces[k], 0.0)
        sides.append(total)
    side = jnp.concatenate(sides, 1)
    square_own, square_other = gather_segments(
        total_over_rows(side[:segment], (1, 2, 4, 8, 16)), my_col
    )
    tops_own, tops_other = gather_segments(
        total_over_rows(side[segment:], (8, 16, 1, 2, 4)), my_col
    )
    raw = spread_columns(first, my_col)
    spread = spread_tops(mine[:block], my_row)

    moved_first = exchanged(row, first_pivots, 0)
    moved = exchanged(exchanged(row, second_pivots, block), first_pivots, 0)
    packed, linv, uinv = factor_two(me, square_own, square_other)
    store, high, low = panels(
        me, jnp.stack([row, moved, moved_first], 1), raw, tops_own, tops_other, packed, uinv
    )
    flat = lambda a: a.reshape(a.shape[0] * cols, width)
    landing = jnp.where(
        (moved != row) & (row >= count), place_of_top(moved % count, my_row, block), -1
    )
    near = place_of_top(source % count, my_row, block)

    def finish(at, others):
        return trailing(
            me, row, landing, at, [flat(a) for a in spread], flat(others), flat(mine), high, low,
            packed, linv, store, cols,
        )

    def usual():
        return finish(jnp.where(far, count + holder * SLOTS + rank, near), gathered)

    def crowded():
        return finish(count + order, lax.psum(collect(local, mine), "prow"))

    return lax.cond(fits, usual, crowded).reshape(matrix.shape)


def solution(mesh):
    in_specs = (P(None, "prow", None, "pcol"), P())
    out_specs = P(None, "prow", None, "pcol")
    return jax.shard_map(
        per_device, mesh=mesh, in_specs=in_specs, out_specs=out_specs, check_vma=False
    )
```

```python
import jax
import jax.numpy as jnp
from jax import lax
from jax.experimental import pallas as pl
from jax.experimental.pallas import tpu as pltpu
from jax.sharding import PartitionSpec as P

BASE = 64
GROUP = 8
LIMIT = 48 * 2**20
SLOTS = 28
X, Z, Y = 4, 8, 4


def exact(a, b):
    return jnp.dot(a, b, precision=lax.Precision.HIGHEST, preferred_element_type=jnp.float32)


def split(a):
    high = a.astype(jnp.bfloat16)
    return high, (a - high.astype(jnp.float32)).astype(jnp.bfloat16)


def triple(a, b):
    dot = lambda x, y: jnp.dot(x, y, preferred_element_type=jnp.float32)
    return dot(a[0], b[0]) + (dot(a[0], b[1]) + dot(a[1], b[0]))


def factor_base(block):
    n = BASE
    tiles = n // 8
    lane = lax.broadcasted_iota(jnp.int32, (8, 128), 1)
    sub = lax.broadcasted_iota(jnp.int32, (8, 128), 0)
    row_id = lax.broadcasted_iota(jnp.int32, (n, n), 0)
    col_id = lax.broadcasted_iota(jnp.int32, (n, n), 1)
    unit = jnp.where(row_id == col_id, 1.0, 0.0).astype(jnp.float32)
    wide = [jnp.concatenate([block, unit], 1), jnp.concatenate([block.T, unit], 1)]
    work = [[w[8 * r:8 * r + 8] for r in range(tiles)] for w in wide]
    lower = [jnp.zeros((8, 128), jnp.float32) for _ in range(tiles)]
    scale = [jnp.zeros((8, 128), jnp.float32) for _ in range(tiles)]
    spread = lambda tile, s: jnp.broadcast_to(tile[s:s + 1, :], (8, 128))
    for first in range(0, n, GROUP):
        cols = [
            {j: {r: jnp.broadcast_to(work[b][r][:, j:j + 1], (8, 128)) for r in range(first // 8, tiles)}
             for j in range(first, first + GROUP)}
            for b in range(2)
        ]
        for k in range(first, first + GROUP):
            kt, ks = divmod(k, 8)
            for b in range(2):
                inv = 1.0 / spread(cols[b][k][kt], ks)
                mult = {r: cols[b][k][r] * inv for r in range(kt, tiles)}
                mult[kt] = jnp.where(sub > ks, mult[kt], 0.0)
                for j in range(k + 1, first + GROUP):
                    across = spread(cols[b][j][kt], ks)
                    for r in range(kt, tiles):
                        cols[b][j][r] = cols[b][j][r] - mult[r] * across
                across = spread(work[b][kt], ks)
                for r in range(kt, tiles):
                    work[b][r] = work[b][r] - mult[r] * across
                if b == 0:
                    for r in range(kt, tiles):
                        lower[r] = jnp.where(lane == k, mult[r], lower[r])
                else:
                    scale[kt] = jnp.where(sub == ks, inv, scale[kt])
    first_work = jnp.concatenate(work[0], 0)
    second_work = jnp.concatenate([work[1][r] * scale[r] for r in range(tiles)], 0)
    packed = jnp.where(row_id <= col_id, first_work[:, :n], jnp.concatenate(lower, 0)[:, :n])
    lower_inv = first_work[:, n:]
    upper_inv = second_work[:, n:].T
    return packed, lower_inv, upper_inv

def join(a, b, c, d):
    return jnp.concatenate([jnp.concatenate([a, b], 1), jnp.concatenate([c, d], 1)], 0)

def factor(square):
    size = square.shape[0]
    if size == BASE:
        return factor_base(square)
    h = size // 2
    p1, l1, u1 = factor(square[:h, :h])
    ur = exact(l1, square[:h, h:])
    ll = exact(square[h:, :h], u1)
    p2, l2, u2 = factor(square[h:, h:] - exact(ll, ur))
    z = jnp.zeros((h, h), jnp.float32)
    return (join(p1, ur, ll, p2), join(l1, z, -exact(l2, exact(ll, l1)), l2),
            join(u1, -exact(u1, exact(ur, u2)), z, u2))

def factor_kernel(d_ref, packed_ref, linv_ref, uinv_ref):
    h = d_ref.shape[0] // 2
    p1, l1, u1 = factor(d_ref[:h, :h])
    ur = exact(l1, d_ref[:h, h:])
    ll = exact(d_ref[h:, :h], u1)
    packed_ref[:h, :h] = p1
    packed_ref[:h, h:] = ur
    packed_ref[h:, :h] = ll
    linv_ref[0] = l1
    uinv_ref[0] = u1
    p2, l2, u2 = factor(d_ref[h:, h:] - exact(ll, ur))
    packed_ref[h:, h:] = p2
    linv_ref[1] = l2
    uinv_ref[1] = u2

def place_pieces(me_ref, own_ref, other_ref, part, out_ref):
    per = own_ref.shape[0]
    segment_rows = out_ref.shape[0] // (2 * per)
    size = segment_rows // Z
    for core, ref in ((0, own_ref), (1, other_ref)):
        for turn in range(per):
            segment = lax.rem(me_ref[1] // 2 + turn, per) * 2 + lax.rem(me_ref[1] + core, 2)
            for k in range(Z):
                piece = lax.rem(me_ref[0] + Z - k, Z)
                at = pl.multiple_of(segment * segment_rows + piece * size, size)
                first = (2 * k + part) * size
                out_ref[pl.ds(at, size), :] = ref[turn, first : first + size, :]


def assemble_and_factor(me_ref, own_ref, other_ref, packed_ref, linv_ref, uinv_ref, square):
    place_pieces(me_ref, own_ref, other_ref, 0, square)
    factor_kernel(square, packed_ref, linv_ref, uinv_ref)


def factor_two(me, own, other):
    n = own.shape[2]
    half = jax.ShapeDtypeStruct((2, n // 2, n // 2), jnp.float32)
    smem = pl.BlockSpec(memory_space=pltpu.SMEM)
    vmem = pl.BlockSpec(memory_space=pltpu.VMEM)
    return pl.pallas_call(
        assemble_and_factor,
        out_shape=(jax.ShapeDtypeStruct((n, n), jnp.float32), half, half),
        in_specs=[smem, vmem, vmem],
        out_specs=(vmem, vmem, vmem),
        scratch_shapes=[pltpu.VMEM((n, n), jnp.float32)],
        compiler_params=pltpu.CompilerParams(vmem_limit_bytes=LIMIT),
        cost_estimate=pl.CostEstimate(
            flops=20_000_000_000, bytes_accessed=3 * 2**20, transcendentals=0
        ),
    )(me, own, other)


def panels_kernel(
    me_ref, src_ref, raw_ref, own_ref, other_ref, packed_ref, uinv_ref, store_ref, high_ref,
    low_ref, tops_ref,
):
    n = raw_ref.shape[0]
    h = n // 2
    place_pieces(me_ref, own_ref, other_ref, 1, tops_ref)
    src = src_ref[...]
    row = src[:, 0:1]
    moved = src[:, 1:2]
    moved_first = src[:, 2:3]
    column = lax.broadcasted_iota(jnp.int32, (n, n), 1)
    pick = jnp.where((moved == column) & (moved != row), 1.0, 0.0).astype(jnp.float32)
    raw = raw_ref[...]
    both = jnp.where(moved != row, exact(pick, tops_ref[...]), raw)
    pick = jnp.where((moved_first == column) & (moved_first != row), 1.0, 0.0)[:, :h]
    first = jnp.where(
        moved_first != row, exact(pick.astype(jnp.float32), tops_ref[:h, :h]), raw[:, :h]
    )
    store_ref[0] = exact(first, uinv_ref[0])
    left = exact(both[:, :h], uinv_ref[0])
    right = exact(both[:, h:] - exact(left, packed_ref[:h, h:]), uinv_ref[1])
    store_ref[1] = right
    high, low = split(jnp.concatenate([left, right], 1))
    high_ref[...] = high
    low_ref[...] = low


def panels(me, src, raw, own, other, packed, uinv):
    n = raw.shape[0]
    pair = jax.ShapeDtypeStruct((n, n), jnp.bfloat16)
    smem = pl.BlockSpec(memory_space=pltpu.SMEM)
    vmem = pl.BlockSpec(memory_space=pltpu.VMEM)
    return pl.pallas_call(
        panels_kernel,
        out_shape=(jax.ShapeDtypeStruct((2, n, n // 2), jnp.float32), pair, pair),
        in_specs=[smem] + [vmem] * 6,
        out_specs=(vmem, vmem, vmem),
        scratch_shapes=[pltpu.VMEM((n, n), jnp.float32)],
        compiler_params=pltpu.CompilerParams(vmem_limit_bytes=LIMIT),
        cost_estimate=pl.CostEstimate(
            flops=5_000_000_000, bytes_accessed=6 * 2**20, transcendentals=0
        ),
    )(me, src, raw, own, other, packed, uinv)


def pick_kernel(cols, wanted_ref, index_ref, mine_ref, raw_ref, sent_ref, *refs):
    out_refs, (held, sem) = refs[:-2], refs[-2:]
    lanes = held.shape[2]
    part = lambda i: pl.ds(i * lanes, lanes)
    copies = [
        pltpu.make_async_copy(mine_ref.at[:, part(i)], held.at[i], sem.at[i]) for i in range(2)
    ]
    for copy in copies:
        copy.start()
    rows, depth = index_ref.shape[0], raw_ref.shape[0]
    column = lax.broadcasted_iota(jnp.int32, (rows, depth), 1)
    pick = jnp.where(index_ref[...] == column, 1.0, 0.0).astype(jnp.float32)
    for copy in copies:
        copy.wait()
    for i in range(2):
        raw_ref[:, part(i)] = held[i, pl.ds(0, depth, stride=cols), :]
        for k in range(wanted_ref.shape[0]):
            source = pl.ds(pl.multiple_of(wanted_ref[k] * cols, cols), cols)
            sent_ref[pl.ds(k * cols, cols), part(i)] = held[i, source, :]
    picked = exact(pick, raw_ref[...])
    step = rows // len(out_refs)
    for k, ref in enumerate(out_refs):
        ref[...] = picked[k * step : (k + 1) * step]


def pick_pieces(wanted, index, mine, cols, pieces):
    rows, width = mine.shape
    smem = pl.BlockSpec(memory_space=pltpu.SMEM)
    vmem = pl.BlockSpec(memory_space=pltpu.VMEM)
    shape = lambda n: jax.ShapeDtypeStruct((n, width), jnp.float32)
    body = lambda *refs: pick_kernel(cols, *refs)
    return pl.pallas_call(
        body,
        out_shape=(shape(rows // cols), shape(wanted.shape[0] * cols))
        + (shape(index.shape[0] // pieces),) * pieces,
        in_specs=[smem, vmem, pl.BlockSpec(memory_space=pl.ANY)],
        out_specs=(vmem,) * (2 + pieces),
        scratch_shapes=[
            pltpu.VMEM((width // 128, rows, 128), jnp.float32),
            pltpu.SemaphoreType.DMA((2,)),
        ],
        compiler_params=pltpu.CompilerParams(vmem_limit_bytes=LIMIT),
    )(wanted, index, mine)


def collect_kernel(local_ref, mine_ref, out_ref):
    def one(s, _):
        at = local_ref[s]

        @pl.when(at >= 0)
        def _():
            out_ref[s] = mine_ref[at]

        @pl.when(at < 0)
        def _():
            out_ref[s] = jnp.zeros_like(out_ref[s])

        return 0

    lax.fori_loop(0, local_ref.shape[0], one, 0)


def collect(local, mine):
    vmem = pl.BlockSpec(memory_space=pltpu.VMEM)
    return pl.pallas_call(
        collect_kernel,
        out_shape=jax.ShapeDtypeStruct((local.shape[0],) + mine.shape[1:], jnp.float32),
        in_specs=[pl.BlockSpec(memory_space=pltpu.SMEM), vmem],
        out_specs=vmem,
        compiler_params=pltpu.CompilerParams(vmem_limit_bytes=LIMIT),
    )(local, mine)


def trailing_kernel(
    cols, me_ref, to_ref, from_ref, at_ref, rows_ref, mine_ref, high_ref, low_ref, packed_ref,
    linv_ref, store_ref, out_ref, work, top, uppers, right_high, right_low, moved, in_sem,
    moved_sem, out_sem,
):
    rows = at_ref.shape[0]
    h = rows // 2
    lanes = top.shape[2]
    halves = range(top.shape[0])
    part = lambda i: pl.ds(i * lanes, lanes)
    moved_copy = pltpu.make_async_copy(rows_ref, moved, moved_sem)
    in_copies = [
        pltpu.make_async_copy(mine_ref.at[:, part(i)], work.at[i], in_sem.at[i]) for i in halves
    ]
    for copy in [moved_copy] + in_copies:
        copy.start()

    def load(ref, first, count, j):
        at = pl.ds(first * cols + j, count, stride=cols)
        return jnp.concatenate([ref[i, at, :] for i in halves], 1)

    def store(ref, first, count, j, value):
        at = pl.ds(first * cols + j, count, stride=cols)
        for i in halves:
            ref[i, at, :] = value[:, i * lanes : (i + 1) * lanes]

    def place(ref, target, source):
        target = pl.ds(pl.multiple_of(target * cols, cols), cols)
        source = pl.ds(pl.multiple_of(source * cols, cols), cols)
        for i in halves:
            ref[i, target, :] = moved[source, part(i)]

    def place_top(t, _):
        for k in range(16):
            place(top, t * 16 + k, at_ref[t * 16 + k])
        return 0

    def place_work(t, _):
        place(work, to_ref[t], from_ref[t])
        return 0

    inverse = [split(linv_ref[k]) for k in range(2)]
    corner = split(packed_ref[h:, :h])
    my_row = me_ref[0]
    my_col = me_ref[1]
    moved_copy.wait()
    lax.fori_loop(0, rows // 16, place_top, 0)
    for copy in in_copies:
        copy.wait()
    lax.fori_loop(0, me_ref[2], place_work, 0)
    for j in range(cols):
        upper = triple(inverse[0], split(load(top, 0, h, j)))
        upper_pair = split(upper)
        second = load(top, h, h, j) - triple(corner, upper_pair)
        second = triple(inverse[1], split(second))
        second_pair = split(second)
        for ref, pieces in ((right_high, (upper_pair[0], second_pair[0])),
                            (right_low, (upper_pair[1], second_pair[1]))):
            for k, piece in enumerate(pieces):
                ref[j, k * h : k * h + h, :] = piece
        uppers[0, j] = upper
        uppers[1, j] = second

    def update(first, j):
        at = slice(first, first + h)
        change = triple((high_ref[at, :], low_ref[at, :]), (right_high[j], right_low[j]))
        store(work, first, h, j, load(work, first, h, j) - change)

    out_copies = []
    for first in range(0, rows, h):
        at = slice(first, first + h)
        if first == 0:

            @pl.when(my_row >= 2)
            def _():
                for j in range(cols):
                    update(0, j)

            for k in range(2):

                @pl.when(my_row == k)
                def _():
                    for j in range(cols):
                        store(work, 0, h, j, uppers[k, j])

        else:
            for j in range(cols):
                update(first, j)
        for k in range(2):

            @pl.when(my_col == k)
            def _():
                store(work, first, h, 0, store_ref[k, at, :])
                if first == 0:
                    for i in range(k + 1):

                        @pl.when(my_row == i)
                        def _():
                            store(
                                work, 0, h, 0,
                                packed_ref[i * h : i * h + h, k * h : k * h + h],
                            )

        span = pl.ds(first * cols, h * cols)
        for i in halves:
            copy = pltpu.make_async_copy(
                work.at[i, span], out_ref.at[span, part(i)], out_sem.at[i, first // h]
            )
            copy.start()
            out_copies.append(copy)
    for copy in out_copies:
        copy.wait()


def trailing(me, to, source, at, moved, mine, high, low, packed, linv, store, cols):
    smem = pl.BlockSpec(memory_space=pltpu.SMEM)
    vmem = pl.BlockSpec(memory_space=pltpu.VMEM)
    hbm = pl.BlockSpec(memory_space=pl.ANY)
    rows = at.shape[0]
    width = mine.shape[1]
    wide = pltpu.VMEM((width // 128, rows * cols, 128), jnp.float32)
    right = pltpu.VMEM((cols, rows, width), jnp.bfloat16)
    body = lambda *refs: trailing_kernel(cols, *refs)
    return pl.pallas_call(
        body,
        out_shape=jax.ShapeDtypeStruct(mine.shape, jnp.float32),
        in_specs=[smem] * 4 + [hbm] * 2 + [vmem] * 5,
        out_specs=hbm,
        scratch_shapes=[
            wide, wide,
            pltpu.VMEM((2, cols, rows // 2, width), jnp.float32),
            right, right,
            pltpu.VMEM(moved.shape, jnp.float32),
            pltpu.SemaphoreType.DMA((2,)),
            pltpu.SemaphoreType.DMA,
            pltpu.SemaphoreType.DMA((2, 2)),
        ],
        compiler_params=pltpu.CompilerParams(vmem_limit_bytes=LIMIT),
    )(me, to, source, at, moved, mine, high, low, packed, linv, store)


def turn_columns(value, turn):
    return lax.ppermute(value, "pcol", [(q, (q + turn) % 8) for q in range(8)])


def spread_columns(first, my_col):
    y = my_col // 2
    up, down = turn_columns(first, 2), turn_columns(first, -2)
    held = jnp.where(y == 0, first, jnp.where(y == 1, up, down))
    return held, turn_columns(held, 2)


def join_columns(held, turned, my_col):
    held = jnp.where(my_col // 2 == 2, turned, held)
    other = lax.ppermute(held, "pcol", [(q, q ^ 1) for q in range(8)])
    even = my_col % 2 == 0
    return jnp.concatenate([jnp.where(even, held, other), jnp.where(even, other, held)], 1)


def along_z(value, turn):
    pairs = [(x * Z + z, x * Z + (z + turn) % Z) for x in range(X) for z in range(Z)]
    return lax.ppermute(value, "prow", pairs)


def gather_segments(piece, my_col):
    held = [piece] + [
        lax.ppermute(piece, "pcol", [((q + 2 * k) % 8, q) for q in range(8)]) for k in range(1, Y)
    ]
    own = jnp.stack(held)
    return own, lax.ppermute(own, "pcol", [(q, q ^ 1) for q in range(8)])


def along_x(value, turn):
    pairs = [(x * Z + z, (x + turn) % X * Z + z) for x in range(X) for z in range(Z)]
    return lax.ppermute(value, "prow", pairs)


def total_over_rows(value, my_row):
    z = my_row % Z
    parts = value.reshape(Z, value.shape[0] // Z, value.shape[1])
    parts = lax.dynamic_slice_in_dim(jnp.concatenate([parts, parts], 0), z, Z, 0)
    total = parts[0] + sum([along_z(parts[k], k) for k in range(1, Z)])
    total = total + sum([along_x(total, k) for k in range(1, X)])
    return jnp.concatenate([total] + [along_z(total, k) for k in range(1, Z)], 0)


def deal_planes(tops, my_row):
    plane = tops.shape[0] // X
    sent = [
        lax.ppermute(tops[k * plane : (k + 1) * plane], "prow", [(0, k * Z), (1, k * Z + 1)])
        for k in range(1, X)
    ]
    return jnp.where(my_row // Z == 0, tops[:plane], sum(sent))


def deal_rows(held, my_row):
    per = held.shape[0] // Z
    z = my_row % Z
    held = jnp.where(z == 1, jnp.concatenate([held[per:], held[:per]], 0), held)
    chunks = [held[k * per : (k + 1) * per] for k in range(Z)]
    sent = [chunks[0]] + [along_z(chunks[k], k) for k in range(1, Z)]
    chosen = []
    for start in range(2):
        total = jnp.zeros_like(chunks[0])
        for k in range(Z):
            total = total + jnp.where(z == (start + k) % Z, sent[k], 0.0)
        chosen.append(total)
    return jnp.concatenate(chosen, 0)


def per_device(matrix, pivots):
    prow_count = lax.axis_size("prow")
    pcol_count = lax.axis_size("pcol")
    my_row = lax.axis_index("prow")
    my_col = lax.axis_index("pcol")
    row_count, block, cols, width = matrix.shape
    rows = row_count * block
    mine = matrix.reshape(rows, cols, width)
    me = jnp.stack([my_row, my_col]).astype(jnp.int32)
    offsets = jnp.arange(block, dtype=jnp.int32)
    row = (
        (jnp.arange(row_count, dtype=jnp.int32) * prow_count + my_row)[:, None] * block
        + offsets[None, :]
    ).reshape(rows)
    first_pivots = pivots[:block]
    second_pivots = pivots[block:]
    count = 2 * block

    def exchanged(index, chosen, start):
        match = (index[:, None] == chosen[None, :]) & (index[:, None] >= start + block)
        found = jnp.max(jnp.where(match, offsets[None, :] + start, -1), axis=1)
        return jnp.where(found >= 0, found, index)

    source = jnp.concatenate([first_pivots, exchanged(second_pivots, first_pivots, 0)])
    panel = source // block
    holder = panel % prow_count
    place = panel // prow_count * block + source % block
    local = jnp.where(holder == my_row, place, -1)
    far = source >= count
    order = jnp.arange(count, dtype=jnp.int32)
    before = (holder[:, None] == holder[None, :]) & far[None, :] & (order[None, :] < order[:, None])
    rank = jnp.sum(before.astype(jnp.int32), axis=1)
    fits = jnp.max(jnp.where(far, rank, 0)) < SLOTS
    slots = jnp.arange(SLOTS, dtype=jnp.int32)
    filled = (rank[None, :] == slots[:, None]) & (far & (holder == my_row))[None, :]
    wanted = jnp.sum(jnp.where(filled, place[None, :], 0), axis=1)
    flat = lambda a: a.reshape(a.shape[0] * cols, width)

    planes = deal_planes(mine[:block], my_row)
    segment = count // pcol_count
    tops_local = jnp.where(order // block == my_row, order % block, -1)
    both = jnp.stack([local, tops_local], 0).reshape(2, pcol_count, Z, segment // Z)
    both = both.transpose(1, 2, 0, 3)
    both = lax.dynamic_slice_in_dim(jnp.concatenate([both, both], 0), my_col, pcol_count, 0)
    first, far_rows, *pieces = pick_pieces(
        wanted, both.reshape(2 * count, 1), flat(mine), cols, pcol_count
    )
    planes, first, pieces = lax.optimization_barrier((planes, first, pieces))
    dealt = deal_rows(planes, my_row)
    moved_pieces = [pieces[0]] + [turn_columns(pieces[k], k) for k in range(1, pcol_count)]
    sides = []
    for start in range(2):
        total = jnp.zeros_like(pieces[0])
        for k in range(pcol_count):
            here = my_col == (start + k) % pcol_count
            total = total + jnp.where(here, moved_pieces[k], 0.0)
        sides.append(total)
    side = jnp.concatenate(sides, 1)
    side, first, dealt = lax.optimization_barrier((side, first, dealt))

    sent = jnp.concatenate([far_rows.reshape(SLOTS, cols, width), dealt], 0)
    each = sent.shape[0]
    gathered = lax.all_gather(sent, "prow", tiled=True)

    def place_of_top(index):
        per = block // prow_count
        owner = index % block // per
        return owner * each + SLOTS + index // block * per + index % per

    own, other = gather_segments(total_over_rows(side, my_row), my_col)
    held, turned = spread_columns(first, my_col)

    moved_first = exchanged(row, first_pivots, 0)
    moved = exchanged(exchanged(row, second_pivots, block), first_pivots, 0)
    packed, linv, uinv = factor_two(me, own, other)
    turned, packed = lax.optimization_barrier((turned, packed))
    raw = join_columns(held, turned, my_col)
    store, high, low = panels(
        me, jnp.stack([row, moved, moved_first], 1), raw, own, other, packed, uinv
    )
    lands = (moved != row) & (row >= count)
    landed = jnp.sum((lands[None, :] & (order[None, :] < order[:, None])).astype(jnp.int32), axis=1)
    listed = lands[None, :] & (landed[None, :] == order[:, None])
    pick_one = lambda value: jnp.sum(jnp.where(listed, value[None, :], 0), axis=1)
    to, origin = pick_one(order), pick_one(place_of_top(moved % count))
    me = jnp.concatenate([me, jnp.sum(lands.astype(jnp.int32))[None]])

    def finish(at, others):
        return trailing(
            me, to, origin, at, flat(others), flat(mine), high, low, packed, linv, store, cols
        )

    def usual():
        return finish(jnp.where(far, holder * each + rank, place_of_top(source % count)), gathered)

    def crowded():
        top = lax.psum(collect(local, mine), "prow")
        return finish(prow_count * each + order, jnp.concatenate([gathered, top], 0))

    return lax.cond(fits, usual, crowded).reshape(matrix.shape)


def solution(mesh):
    in_specs = (P(None, "prow", None, "pcol"), P())
    out_specs = P(None, "prow", None, "pcol")
    return jax.shard_map(
        per_device, mesh=mesh, in_specs=in_specs, out_specs=out_specs, check_vma=False
    )
```

```python
import jax
import jax.numpy as jnp
from jax import lax
from jax.experimental import pallas as pl
from jax.experimental.pallas import tpu as pltpu
from jax.sharding import PartitionSpec as P

BASE = 64
GROUP = 8
LIMIT = 48 * 2**20
SLOTS = 28
X, Z, Y = 4, 8, 4


def exact(a, b):
    return jnp.dot(a, b, precision=lax.Precision.HIGHEST, preferred_element_type=jnp.float32)


def split(a):
    high = a.astype(jnp.bfloat16)
    return high, (a - high.astype(jnp.float32)).astype(jnp.bfloat16)


def triple(a, b):
    dot = lambda x, y: jnp.dot(x, y, preferred_element_type=jnp.float32)
    return dot(a[0], b[0]) + (dot(a[0], b[1]) + dot(a[1], b[0]))


def factor_base(block):
    n = BASE
    tiles = n // 8
    lane = lax.broadcasted_iota(jnp.int32, (8, 128), 1)
    sub = lax.broadcasted_iota(jnp.int32, (8, 128), 0)
    row_id = lax.broadcasted_iota(jnp.int32, (n, n), 0)
    col_id = lax.broadcasted_iota(jnp.int32, (n, n), 1)
    unit = jnp.where(row_id == col_id, 1.0, 0.0).astype(jnp.float32)
    wide = [jnp.concatenate([block, unit], 1), jnp.concatenate([block.T, unit], 1)]
    work = [[w[8 * r:8 * r + 8] for r in range(tiles)] for w in wide]
    lower = [jnp.zeros((8, 128), jnp.float32) for _ in range(tiles)]
    scale = [jnp.zeros((8, 128), jnp.float32) for _ in range(tiles)]
    spread = lambda tile, s: jnp.broadcast_to(tile[s:s + 1, :], (8, 128))
    for first in range(0, n, GROUP):
        cols = [
            {j: {r: jnp.broadcast_to(work[b][r][:, j:j + 1], (8, 128)) for r in range(first // 8, tiles)}
             for j in range(first, first + GROUP)}
            for b in range(2)
        ]
        for k in range(first, first + GROUP):
            kt, ks = divmod(k, 8)
            for b in range(2):
                inv = 1.0 / spread(cols[b][k][kt], ks)
                mult = {r: cols[b][k][r] * inv for r in range(kt, tiles)}
                mult[kt] = jnp.where(sub > ks, mult[kt], 0.0)
                for j in range(k + 1, first + GROUP):
                    across = spread(cols[b][j][kt], ks)
                    for r in range(kt, tiles):
                        cols[b][j][r] = cols[b][j][r] - mult[r] * across
                across = spread(work[b][kt], ks)
                for r in range(kt, tiles):
                    work[b][r] = work[b][r] - mult[r] * across
                if b == 0:
                    for r in range(kt, tiles):
                        lower[r] = jnp.where(lane == k, mult[r], lower[r])
                else:
                    scale[kt] = jnp.where(sub == ks, inv, scale[kt])
    first_work = jnp.concatenate(work[0], 0)
    second_work = jnp.concatenate([work[1][r] * scale[r] for r in range(tiles)], 0)
    packed = jnp.where(row_id <= col_id, first_work[:, :n], jnp.concatenate(lower, 0)[:, :n])
    lower_inv = first_work[:, n:]
    upper_inv = second_work[:, n:].T
    return packed, lower_inv, upper_inv

def join(a, b, c, d):
    return jnp.concatenate([jnp.concatenate([a, b], 1), jnp.concatenate([c, d], 1)], 0)

def factor(square):
    size = square.shape[0]
    if size == BASE:
        return factor_base(square)
    h = size // 2
    p1, l1, u1 = factor(square[:h, :h])
    ur = exact(l1, square[:h, h:])
    ll = exact(square[h:, :h], u1)
    p2, l2, u2 = factor(square[h:, h:] - exact(ll, ur))
    z = jnp.zeros((h, h), jnp.float32)
    return (join(p1, ur, ll, p2), join(l1, z, -exact(l2, exact(ll, l1)), l2),
            join(u1, -exact(u1, exact(ur, u2)), z, u2))

def factor_kernel(d_ref, packed_ref, linv_ref, uinv_ref):
    h = d_ref.shape[0] // 2
    p1, l1, u1 = factor(d_ref[:h, :h])
    ur = exact(l1, d_ref[:h, h:])
    ll = exact(d_ref[h:, :h], u1)
    packed_ref[:h, :h] = p1
    packed_ref[:h, h:] = ur
    packed_ref[h:, :h] = ll
    linv_ref[0] = l1
    uinv_ref[0] = u1
    p2, l2, u2 = factor(d_ref[h:, h:] - exact(ll, ur))
    packed_ref[h:, h:] = p2
    linv_ref[1] = l2
    uinv_ref[1] = u2

def place_pieces(me_ref, own_ref, other_ref, part, out_ref):
    per = own_ref.shape[0]
    segment_rows = out_ref.shape[0] // (2 * per)
    size = segment_rows // Z
    for core, ref in ((0, own_ref), (1, other_ref)):
        for turn in range(per):
            segment = lax.rem(me_ref[1] // 2 + turn, per) * 2 + lax.rem(me_ref[1] + core, 2)
            for k in range(Z):
                piece = lax.rem(me_ref[0] + Z - k, Z)
                at = pl.multiple_of(segment * segment_rows + piece * size, size)
                first = (2 * k + part) * size
                out_ref[pl.ds(at, size), :] = ref[turn, first : first + size, :]


def assemble_and_factor(me_ref, own_ref, other_ref, packed_ref, linv_ref, uinv_ref, square):
    place_pieces(me_ref, own_ref, other_ref, 0, square)
    factor_kernel(square, packed_ref, linv_ref, uinv_ref)


def factor_two(me, own, other):
    n = own.shape[2]
    half = jax.ShapeDtypeStruct((2, n // 2, n // 2), jnp.float32)
    smem = pl.BlockSpec(memory_space=pltpu.SMEM)
    vmem = pl.BlockSpec(memory_space=pltpu.VMEM)
    return pl.pallas_call(
        assemble_and_factor,
        out_shape=(jax.ShapeDtypeStruct((n, n), jnp.float32), half, half),
        in_specs=[smem, vmem, vmem],
        out_specs=(vmem, vmem, vmem),
        scratch_shapes=[pltpu.VMEM((n, n), jnp.float32)],
        compiler_params=pltpu.CompilerParams(vmem_limit_bytes=LIMIT),
        cost_estimate=pl.CostEstimate(
            flops=20_000_000_000, bytes_accessed=3 * 2**20, transcendentals=0
        ),
    )(me, own, other)


def panels_kernel(
    me_ref, src_ref, raw_ref, own_ref, other_ref, packed_ref, uinv_ref, store_ref, high_ref,
    low_ref, tops_ref,
):
    n = raw_ref.shape[0]
    h = n // 2
    place_pieces(me_ref, own_ref, other_ref, 1, tops_ref)
    src = src_ref[...]
    row = src[:, 0:1]
    moved = src[:, 1:2]
    moved_first = src[:, 2:3]
    column = lax.broadcasted_iota(jnp.int32, (n, n), 1)
    pick = jnp.where((moved == column) & (moved != row), 1.0, 0.0).astype(jnp.float32)
    raw = raw_ref[...]
    both = jnp.where(moved != row, exact(pick, tops_ref[...]), raw)
    pick = jnp.where((moved_first == column) & (moved_first != row), 1.0, 0.0)[:, :h]
    first = jnp.where(
        moved_first != row, exact(pick.astype(jnp.float32), tops_ref[:h, :h]), raw[:, :h]
    )
    store_ref[0] = exact(first, uinv_ref[0])
    left = exact(both[:, :h], uinv_ref[0])
    right = exact(both[:, h:] - exact(left, packed_ref[:h, h:]), uinv_ref[1])
    store_ref[1] = right
    high, low = split(jnp.concatenate([left, right], 1))
    high_ref[...] = high
    low_ref[...] = low


def panels(me, src, raw, own, other, packed, uinv):
    n = raw.shape[0]
    pair = jax.ShapeDtypeStruct((n, n), jnp.bfloat16)
    smem = pl.BlockSpec(memory_space=pltpu.SMEM)
    vmem = pl.BlockSpec(memory_space=pltpu.VMEM)
    return pl.pallas_call(
        panels_kernel,
        out_shape=(jax.ShapeDtypeStruct((2, n, n // 2), jnp.float32), pair, pair),
        in_specs=[smem] + [vmem] * 6,
        out_specs=(vmem, vmem, vmem),
        scratch_shapes=[pltpu.VMEM((n, n), jnp.float32)],
        compiler_params=pltpu.CompilerParams(vmem_limit_bytes=LIMIT),
        cost_estimate=pl.CostEstimate(
            flops=5_000_000_000, bytes_accessed=6 * 2**20, transcendentals=0
        ),
    )(me, src, raw, own, other, packed, uinv)


def pick_kernel(cols, wanted_ref, index_ref, mine_ref, raw_ref, sent_ref, *refs):
    out_refs, (held, sem) = refs[:-2], refs[-2:]
    lanes = held.shape[2]
    part = lambda i: pl.ds(i * lanes, lanes)
    copies = [
        pltpu.make_async_copy(mine_ref.at[:, part(i)], held.at[i], sem.at[i]) for i in range(2)
    ]
    for copy in copies:
        copy.start()
    rows, depth = index_ref.shape[0], raw_ref.shape[0]
    column = lax.broadcasted_iota(jnp.int32, (rows, depth), 1)
    pick = jnp.where(index_ref[...] == column, 1.0, 0.0).astype(jnp.float32)
    for copy in copies:
        copy.wait()
    for i in range(2):
        raw_ref[:, part(i)] = held[i, pl.ds(0, depth, stride=cols), :]
        for k in range(wanted_ref.shape[0]):
            source = pl.ds(pl.multiple_of(wanted_ref[k] * cols, cols), cols)
            sent_ref[pl.ds(k * cols, cols), part(i)] = held[i, source, :]
    picked = exact(pick, raw_ref[...])
    step = rows // len(out_refs)
    for k, ref in enumerate(out_refs):
        ref[...] = picked[k * step : (k + 1) * step]


def pick_pieces(wanted, index, mine, cols, pieces):
    rows, width = mine.shape
    smem = pl.BlockSpec(memory_space=pltpu.SMEM)
    vmem = pl.BlockSpec(memory_space=pltpu.VMEM)
    shape = lambda n: jax.ShapeDtypeStruct((n, width), jnp.float32)
    body = lambda *refs: pick_kernel(cols, *refs)
    return pl.pallas_call(
        body,
        out_shape=(shape(rows // cols), shape(wanted.shape[0] * cols))
        + (shape(index.shape[0] // pieces),) * pieces,
        in_specs=[smem, vmem, pl.BlockSpec(memory_space=pl.ANY)],
        out_specs=(vmem,) * (2 + pieces),
        scratch_shapes=[
            pltpu.VMEM((width // 128, rows, 128), jnp.float32),
            pltpu.SemaphoreType.DMA((2,)),
        ],
        compiler_params=pltpu.CompilerParams(vmem_limit_bytes=LIMIT),
    )(wanted, index, mine)


def collect_kernel(local_ref, mine_ref, out_ref):
    def one(s, _):
        at = local_ref[s]

        @pl.when(at >= 0)
        def _():
            out_ref[s] = mine_ref[at]

        @pl.when(at < 0)
        def _():
            out_ref[s] = jnp.zeros_like(out_ref[s])

        return 0

    lax.fori_loop(0, local_ref.shape[0], one, 0)


def collect(local, mine):
    vmem = pl.BlockSpec(memory_space=pltpu.VMEM)
    return pl.pallas_call(
        collect_kernel,
        out_shape=jax.ShapeDtypeStruct((local.shape[0],) + mine.shape[1:], jnp.float32),
        in_specs=[pl.BlockSpec(memory_space=pltpu.SMEM), vmem],
        out_specs=vmem,
        compiler_params=pltpu.CompilerParams(vmem_limit_bytes=LIMIT),
    )(local, mine)


def trailing_kernel(
    cols, me_ref, to_ref, from_ref, at_ref, rows_ref, mine_ref, high_ref, low_ref, packed_ref,
    linv_ref, store_ref, out_ref, work, top, uppers, right_high, right_low, moved, in_sem,
    moved_sem, out_sem,
):
    rows = at_ref.shape[0]
    h = rows // 2
    lanes = top.shape[2]
    halves = range(top.shape[0])
    part = lambda i: pl.ds(i * lanes, lanes)
    moved_copy = pltpu.make_async_copy(rows_ref, moved, moved_sem)
    in_copies = [
        pltpu.make_async_copy(mine_ref.at[:, part(i)], work.at[i], in_sem.at[i]) for i in halves
    ]
    for copy in [moved_copy] + in_copies:
        copy.start()

    def load(ref, first, count, j):
        at = pl.ds(first * cols + j, count, stride=cols)
        return jnp.concatenate([ref[i, at, :] for i in halves], 1)

    def store(ref, first, count, j, value):
        at = pl.ds(first * cols + j, count, stride=cols)
        for i in halves:
            ref[i, at, :] = value[:, i * lanes : (i + 1) * lanes]

    def place(ref, target, source):
        target = pl.ds(pl.multiple_of(target * cols, cols), cols)
        source = pl.ds(pl.multiple_of(source * cols, cols), cols)
        for i in halves:
            ref[i, target, :] = moved[source, part(i)]

    def place_top(t, _):
        for k in range(16):
            place(top, t * 16 + k, at_ref[t * 16 + k])
        return 0

    def place_work(t, _):
        place(work, to_ref[t], from_ref[t])
        return 0

    inverse = [split(linv_ref[k]) for k in range(2)]
    corner = split(packed_ref[h:, :h])
    my_row = me_ref[0]
    my_col = me_ref[1]
    moved_copy.wait()
    lax.fori_loop(0, rows // 16, place_top, 0)
    for copy in in_copies:
        copy.wait()
    lax.fori_loop(0, me_ref[2], place_work, 0)
    for j in range(cols):
        upper = triple(inverse[0], split(load(top, 0, h, j)))
        upper_pair = split(upper)
        second = load(top, h, h, j) - triple(corner, upper_pair)
        second = triple(inverse[1], split(second))
        second_pair = split(second)
        for ref, pieces in ((right_high, (upper_pair[0], second_pair[0])),
                            (right_low, (upper_pair[1], second_pair[1]))):
            for k, piece in enumerate(pieces):
                ref[j, k * h : k * h + h, :] = piece
        uppers[0, j] = upper
        uppers[1, j] = second

    def update(first, j):
        at = slice(first, first + h)
        change = triple((high_ref[at, :], low_ref[at, :]), (right_high[j], right_low[j]))
        store(work, first, h, j, load(work, first, h, j) - change)

    out_copies = []
    for first in range(0, rows, h):
        at = slice(first, first + h)
        if first == 0:

            @pl.when(my_row >= 2)
            def _():
                for j in range(cols):
                    update(0, j)

            for k in range(2):

                @pl.when(my_row == k)
                def _():
                    for j in range(cols):
                        store(work, 0, h, j, uppers[k, j])

        else:
            for j in range(cols):
                update(first, j)
        for k in range(2):

            @pl.when(my_col == k)
            def _():
                store(work, first, h, 0, store_ref[k, at, :])
                if first == 0:
                    for i in range(k + 1):

                        @pl.when(my_row == i)
                        def _():
                            store(
                                work, 0, h, 0,
                                packed_ref[i * h : i * h + h, k * h : k * h + h],
                            )

        span = pl.ds(first * cols, h * cols)
        for i in halves:
            copy = pltpu.make_async_copy(
                work.at[i, span], out_ref.at[span, part(i)], out_sem.at[i, first // h]
            )
            copy.start()
            out_copies.append(copy)
    for copy in out_copies:
        copy.wait()


def trailing(me, to, source, at, moved, mine, high, low, packed, linv, store, cols):
    smem = pl.BlockSpec(memory_space=pltpu.SMEM)
    vmem = pl.BlockSpec(memory_space=pltpu.VMEM)
    hbm = pl.BlockSpec(memory_space=pl.ANY)
    rows = at.shape[0]
    width = mine.shape[1]
    wide = pltpu.VMEM((width // 128, rows * cols, 128), jnp.float32)
    right = pltpu.VMEM((cols, rows, width), jnp.bfloat16)
    body = lambda *refs: trailing_kernel(cols, *refs)
    return pl.pallas_call(
        body,
        out_shape=jax.ShapeDtypeStruct(mine.shape, jnp.float32),
        in_specs=[smem] * 4 + [hbm] * 2 + [vmem] * 5,
        out_specs=hbm,
        scratch_shapes=[
            wide, wide,
            pltpu.VMEM((2, cols, rows // 2, width), jnp.float32),
            right, right,
            pltpu.VMEM(moved.shape, jnp.float32),
            pltpu.SemaphoreType.DMA((2,)),
            pltpu.SemaphoreType.DMA,
            pltpu.SemaphoreType.DMA((2, 2)),
        ],
        compiler_params=pltpu.CompilerParams(vmem_limit_bytes=LIMIT),
    )(me, to, source, at, moved, mine, high, low, packed, linv, store)


def turn_columns(value, turn):
    return lax.ppermute(value, "pcol", [(q, (q + turn) % 8) for q in range(8)])


def spread_columns(first, my_col):
    y = my_col // 2
    up, down = turn_columns(first, 2), turn_columns(first, -2)
    return jnp.where(y == 0, first, jnp.where(y == 1, up, down))


def join_columns(held, turned, my_col):
    held = jnp.where(my_col // 2 == 2, turned, held)
    other = lax.ppermute(held, "pcol", [(q, q ^ 1) for q in range(8)])
    even = my_col % 2 == 0
    return jnp.concatenate([jnp.where(even, held, other), jnp.where(even, other, held)], 1)


def along_z(value, turn):
    pairs = [(x * Z + z, x * Z + (z + turn) % Z) for x in range(X) for z in range(Z)]
    return lax.ppermute(value, "prow", pairs)


def gather_segments(piece, my_col):
    held = [piece] + [
        lax.ppermute(piece, "pcol", [((q + 2 * k) % 8, q) for q in range(8)]) for k in range(1, Y)
    ]
    own = jnp.stack(held)
    return own, lax.ppermute(own, "pcol", [(q, q ^ 1) for q in range(8)])


def along_x(value, turn):
    pairs = [(x * Z + z, (x + turn) % X * Z + z) for x in range(X) for z in range(Z)]
    return lax.ppermute(value, "prow", pairs)


def total_over_rows(value, my_row):
    z = my_row % Z
    parts = value.reshape(Z, value.shape[0] // Z, value.shape[1])
    parts = lax.dynamic_slice_in_dim(jnp.concatenate([parts, parts], 0), z, Z, 0)
    total = parts[0] + sum([along_z(parts[k], k) for k in range(1, Z)])
    total = total + sum([along_x(total, k) for k in range(1, X)])
    return jnp.concatenate([total] + [along_z(total, k) for k in range(1, Z)], 0)


def deal_planes(tops, my_row):
    plane = tops.shape[0] // X
    sent = [
        lax.ppermute(tops[k * plane : (k + 1) * plane], "prow", [(0, k * Z), (1, k * Z + 1)])
        for k in range(1, X)
    ]
    return jnp.where(my_row // Z == 0, tops[:plane], sum(sent))


def deal_rows(held, my_row):
    per = held.shape[0] // Z
    z = my_row % Z
    held = jnp.where(z == 1, jnp.concatenate([held[per:], held[:per]], 0), held)
    chunks = [held[k * per : (k + 1) * per] for k in range(Z)]
    sent = [chunks[0]] + [along_z(chunks[k], k) for k in range(1, Z)]
    chosen = []
    for start in range(2):
        total = jnp.zeros_like(chunks[0])
        for k in range(Z):
            total = total + jnp.where(z == (start + k) % Z, sent[k], 0.0)
        chosen.append(total)
    return jnp.concatenate(chosen, 0)


def per_device(matrix, pivots):
    prow_count = lax.axis_size("prow")
    pcol_count = lax.axis_size("pcol")
    my_row = lax.axis_index("prow")
    my_col = lax.axis_index("pcol")
    row_count, block, cols, width = matrix.shape
    rows = row_count * block
    mine = matrix.reshape(rows, cols, width)
    me = jnp.stack([my_row, my_col]).astype(jnp.int32)
    offsets = jnp.arange(block, dtype=jnp.int32)
    row = (
        (jnp.arange(row_count, dtype=jnp.int32) * prow_count + my_row)[:, None] * block
        + offsets[None, :]
    ).reshape(rows)
    first_pivots = pivots[:block]
    second_pivots = pivots[block:]
    count = 2 * block

    def exchanged(index, chosen, start):
        match = (index[:, None] == chosen[None, :]) & (index[:, None] >= start + block)
        found = jnp.max(jnp.where(match, offsets[None, :] + start, -1), axis=1)
        return jnp.where(found >= 0, found, index)

    source = jnp.concatenate([first_pivots, exchanged(second_pivots, first_pivots, 0)])
    panel = source // block
    holder = panel % prow_count
    place = panel // prow_count * block + source % block
    local = jnp.where(holder == my_row, place, -1)
    far = source >= count
    order = jnp.arange(count, dtype=jnp.int32)
    before = (holder[:, None] == holder[None, :]) & far[None, :] & (order[None, :] < order[:, None])
    rank = jnp.sum(before.astype(jnp.int32), axis=1)
    fits = jnp.max(jnp.where(far, rank, 0)) < SLOTS
    slots = jnp.arange(SLOTS, dtype=jnp.int32)
    filled = (rank[None, :] == slots[:, None]) & (far & (holder == my_row))[None, :]
    wanted = jnp.sum(jnp.where(filled, place[None, :], 0), axis=1)
    flat = lambda a: a.reshape(a.shape[0] * cols, width)

    planes = deal_planes(mine[:block], my_row)
    segment = count // pcol_count
    tops_local = jnp.where(order // block == my_row, order % block, -1)
    both = jnp.stack([local, tops_local], 0).reshape(2, pcol_count, Z, segment // Z)
    both = both.transpose(1, 2, 0, 3)
    both = lax.dynamic_slice_in_dim(jnp.concatenate([both, both], 0), my_col, pcol_count, 0)
    first, far_rows, *pieces = pick_pieces(
        wanted, both.reshape(2 * count, 1), flat(mine), cols, pcol_count
    )
    planes, first, pieces = lax.optimization_barrier((planes, first, pieces))
    dealt = deal_rows(planes, my_row)
    moved_pieces = [pieces[0]] + [turn_columns(pieces[k], k) for k in range(1, pcol_count)]
    sides = []
    for start in range(2):
        total = jnp.zeros_like(pieces[0])
        for k in range(pcol_count):
            here = my_col == (start + k) % pcol_count
            total = total + jnp.where(here, moved_pieces[k], 0.0)
        sides.append(total)
    side = jnp.concatenate(sides, 1)
    side, first, dealt = lax.optimization_barrier((side, first, dealt))

    sent = jnp.concatenate([far_rows.reshape(SLOTS, cols, width), dealt], 0)
    each = sent.shape[0]
    gathered = lax.all_gather(sent, "prow", tiled=True)

    def place_of_top(index):
        per = block // prow_count
        owner = index % block // per
        return owner * each + SLOTS + index // block * per + index % per

    held = spread_columns(first, my_col)
    total, held = lax.optimization_barrier((total_over_rows(side, my_row), held))
    turned = turn_columns(held, 2)
    own, other = gather_segments(total, my_col)

    moved_first = exchanged(row, first_pivots, 0)
    moved = exchanged(exchanged(row, second_pivots, block), first_pivots, 0)
    packed, linv, uinv = factor_two(me, own, other)
    turned, packed = lax.optimization_barrier((turned, packed))
    raw = join_columns(held, turned, my_col)
    store, high, low = panels(
        me, jnp.stack([row, moved, moved_first], 1), raw, own, other, packed, uinv
    )
    lands = (moved != row) & (row >= count)
    landed = jnp.sum((lands[None, :] & (order[None, :] < order[:, None])).astype(jnp.int32), axis=1)
    listed = lands[None, :] & (landed[None, :] == order[:, None])
    pick_one = lambda value: jnp.sum(jnp.where(listed, value[None, :], 0), axis=1)
    to, origin = pick_one(order), pick_one(place_of_top(moved % count))
    me = jnp.concatenate([me, jnp.sum(lands.astype(jnp.int32))[None]])

    def finish(at, others):
        return trailing(
            me, to, origin, at, flat(others), flat(mine), high, low, packed, linv, store, cols
        )

    def usual():
        return finish(jnp.where(far, holder * each + rank, place_of_top(source % count)), gathered)

    def crowded():
        top = lax.psum(collect(local, mine), "prow")
        return finish(prow_count * each + order, jnp.concatenate([gathered, top], 0))

    return lax.cond(fits, usual, crowded).reshape(matrix.shape)


def solution(mesh):
    in_specs = (P(None, "prow", None, "pcol"), P())
    out_specs = P(None, "prow", None, "pcol")
    return jax.shard_map(
        per_device, mesh=mesh, in_specs=in_specs, out_specs=out_specs, check_vma=False
    )
```
